512 devices in a mesh: rows: 16 (over z, core), rhs: 32 (over y, x).
Axes of the slice: x: 4, y: 8, z: 8, core: 2. Of those that a mesh axis runs over, the one named last changes fastest.
Arguments:
- rhs_blocks: bfloat16 [16, 2048, 4096], P('rows', None, 'rhs'), may hold values from -6 to 6
- left_u: bfloat16 [16, 4, 2048, 256], P('rows', None, 'rhs'), may hold values from -0.375 to 0.375
- left_v: bfloat16 [16, 4, 2048, 256], P('rows', None, 'rhs'), may hold values from -0.125 to 0.125
- tile_ranks: int32 [16, 4], P('rows'), may hold values from 32 to 256
- diag_inverse: bfloat16 [4, 2048, 2048], P(None, 'rows'), may hold values from -8 to 8, as said below
- row_owner: int32 [16], replicated, may hold values from 0 to 15, each once
Outputs:
- solved: bfloat16 [4, 2048, 4096], P(None, 'rows', 'rhs')
- updated: bfloat16 [16, 2048, 4096], P('rows', None, 'rhs')
The draws below stay inside these ranges and needn't reach their ends.
Inputs may be any that keep to these rules, and one draw needn't show every extreme that they name: tile_ranks[s, k] is the rank of the tile in column k of the tile row stored in block s. row_owner[s] is the tile row held in stored block s; every tile row is held exactly once. Each diag_inverse[k] is lower triangular.
All inputs are finite; a program needn't handle non-finite values.
Results may differ from the reference program's by a relative error of at most 0.01.
Values may be sent and summed in bfloat16 or wider, within the bound.
A program may use at most 64 MiB of HBM per device.

```python
import jax
import jax.numpy as jnp
from jax import lax

TS = 2048
RMAX = 256
WIN = 4
NT = 16
NRHS = 4096


def draw_diag_inverse(key, part):
    first_key, second_key = jax.random.split(jax.random.fold_in(key, 17))
    lower = jnp.tril(jnp.ones((TS, TS), jnp.float32), -1)
    off_diag = jax.random.normal(first_key, (WIN, TS, TS), jnp.float32)
    diagonal = jnp.exp(jax.random.uniform(second_key, (WIN, TS), jnp.float32, jnp.log(0.5), jnp.log(2.0)))
    eye_mat = jnp.eye(TS, dtype=jnp.float32)
    whole = off_diag * lower * TS ** (-0.5) + diagonal[:, :, None] * eye_mat
    return whole.astype(jnp.bfloat16)


def place_ends(array, stream_key, smallest, top_value):
    shape = array.shape
    place = [jax.random.randint(jax.random.fold_in(stream_key, axis), (), 0, shape[axis]) for axis in range(len(shape))]
    array = array.at[tuple(place)].set(smallest)
    longest = shape.index(max(shape))
    place[longest] = (place[longest] + 1) % shape[longest]
    return array.at[tuple(place)].set(top_value)


def block_levels(rng, extent, pieces, least, high):
    level, own = 1.0, jax.random.fold_in(rng, 6)
    for axis_at, blocks in pieces:
        heights = jnp.exp(jax.random.uniform(jax.random.fold_in(own, axis_at), (blocks,), jnp.float32, least / len(pieces), high / len(pieces)))
        level = level * jnp.repeat(heights, extent[axis_at] // blocks).reshape([-1 if axis == axis_at else 1 for axis in range(len(extent))])
    return level


def scatter_about(key, shape, scale, reach, cuts=(), held_as=jnp.bfloat16):
    drawn = scale * jax.random.normal(key, shape, jnp.float32)
    if cuts:
        drawn = drawn * block_levels(key, shape, cuts, -0.22, 0.18)
    return jnp.clip(drawn, -reach, reach).astype(held_as)


def setup_inputs(seed: int = 0) -> dict:
    splits = jax.random.split(jax.random.key(seed), 7)
    rhs_blocks = scatter_about(splits[0], (NT, TS, NRHS), 1.0, 6.0, ((0, 16), (2, 32)))
    left_u = scatter_about(splits[1], (NT, WIN, TS, RMAX), RMAX ** -0.5, 0.375, ((0, 16), (2, 32)))
    left_v = scatter_about(splits[2], (NT, WIN, TS, RMAX), TS ** -0.5, 0.125, ((0, 16), (2, 32)))
    tile_ranks = place_ends(jax.random.randint(splits[3], (NT, WIN), RMAX // 8, RMAX + 1), jax.random.fold_in(splits[3], 1), RMAX // 8, RMAX).astype(jnp.int32)
    diag_inverse = draw_diag_inverse(jax.random.fold_in(splits[6], 71), 0)
    row_owner = jax.random.permutation(splits[5], NT).astype(jnp.int32)
    return {"rhs_blocks": rhs_blocks, "left_u": left_u, "left_v": left_v, "tile_ranks": tile_ranks, "diag_inverse": diag_inverse, "row_owner": row_owner}


def reference(rhs_blocks, left_u, left_v, tile_ranks, diag_inverse, row_owner):
    residual = rhs_blocks.astype(jnp.float32)
    stored = jnp.arange(NT, dtype=jnp.int32)
    solved_list = []
    for column in range(WIN):
        owner_index = jnp.sum(jnp.where(row_owner == column, stored, 0)).astype(jnp.int32)
        next_rows = lax.dynamic_index_in_dim(residual, owner_index, 0, keepdims=False).astype(jnp.bfloat16)
        solution = jnp.dot(diag_inverse[column], next_rows, preferred_element_type=jnp.float32).astype(jnp.bfloat16)
        solved_list.append(solution)

        def apply_tile(items):
            u_tile, v_tile, tile_rank, owner_row, old_rows = items
            keep_cols = (jnp.arange(RMAX, dtype=jnp.int32) < tile_rank).astype(v_tile.dtype)
            coeffs = jnp.dot((v_tile * keep_cols).T, solution, preferred_element_type=jnp.float32).astype(jnp.bfloat16)
            update = jnp.dot(u_tile, coeffs, preferred_element_type=jnp.float32)
            return jnp.where(column < owner_row, old_rows - update, old_rows)

        residual = lax.map(apply_tile, (left_u[:, column], left_v[:, column], tile_ranks[:, column], row_owner, residual))
    return jnp.stack(solved_list), residual.astype(jnp.bfloat16)
```

```python
import jax
import jax.numpy as jnp
from jax import lax
from jax.experimental import pallas as pl
from jax.experimental.pallas import tpu as pltpu
from jax.sharding import PartitionSpec as P

MESH = pl.DeviceIdType.MESH
NZ, NY, NX, WIN = 8, 8, 4, 4
FAR_FIRST = (4, 3, 5, 2, 6, 1, 7)
NEAR_FIRST = (1, 7, 2, 6, 3, 5, 4)


def kernel(ranks, owners, rhs, u, v, d, solved, updated, uall, vall, res, stage, sibb, comb, rsb, nag, xag,
           ux_s, ux_r, uy_s, uy_r, vy_s, vy_r, vx_s, vx_r, sib_s, sib_r, rs_s, rs_r, ag_s, ag_r, fw_s, fw_r):
    p, q = lax.axis_index("rows"), lax.axis_index("rhs")
    z, c, y, x = p // 2, p % 2, q // 4, q % 4

    def at_z(dz, core):
        return {"rows": lax.rem(z + dz, NZ) * 2 + core, "rhs": q}

    def at_y(dy):
        return {"rows": p, "rhs": lax.rem(y + dy, NY) * 4 + x}

    def at_x(dx):
        return {"rows": p, "rhs": y * 4 + lax.rem(x + dx, NX)}

    barrier = pltpu.get_barrier_semaphore()
    peers = [at_z(0, 1 - c)]
    peers += [at_z(dz, c) for dz in range(1, NZ)]
    peers += [at_y(1), at_y(NY - 1)] + [at_x(dx) for dx in range(1, NX)]
    for peer in peers:
        pl.semaphore_signal(barrier, inc=1, device_id=peer, device_id_type=MESH)
    pl.semaphore_wait(barrier, len(peers))

    sent = []

    def send(src, dst, s_sem, r_sem, peer):
        copy = pltpu.make_async_remote_copy(
            src_ref=src, dst_ref=dst, send_sem=s_sem, recv_sem=r_sem, device_id=peer, device_id_type=MESH
        )
        copy.start()
        sent.append(copy)

    def arrived(dst, s_sem, r_sem):
        pltpu.make_async_remote_copy(
            src_ref=dst, dst_ref=dst, send_sem=s_sem, recv_sem=r_sem, device_id=at_z(0, 1 - c), device_id_type=MESH
        ).wait_recv()

    def yy(dy):
        return lax.rem(y + dy + NY, NY)

    def gather_step(k, step):
        if step == 0:
            for dx in range(1, NX):
                send(u.at[0, k], uall.at[k, y, x], ux_s.at[k, dx], ux_r.at[k, dx], at_x(dx))
            uall[k, y, x] = u[0, k]
            vall[k, y, x] = v[0, k]
        if step == 1:
            for dx in range(1, NX):
                arrived(uall.at[k, y, lax.rem(x + NX - dx, NX)], ux_s.at[k, dx], ux_r.at[k, dx])
        if 1 <= step <= 4:
            h = step - 1
            if h > 0:
                arrived(uall.at[k, yy(-h)], uy_s.at[k, 0, h], uy_r.at[k, 0, h])
                arrived(uall.at[k, yy(h)], uy_s.at[k, 1, h], uy_r.at[k, 1, h])
            up, down = (uall.at[k, yy(-h)], uall.at[k, yy(h)])
            if h == 3:
                up, down = (up.at[pl.ds(0, 2)], down.at[pl.ds(2, 2)])
            send(up, up, uy_s.at[k, 0, h + 1], uy_r.at[k, 0, h + 1], at_y(1))
            send(down, down, uy_s.at[k, 1, h + 1], uy_r.at[k, 1, h + 1], at_y(NY - 1))
        if step == 5:
            arrived(uall.at[k, yy(4), pl.ds(0, 2)], uy_s.at[k, 0, 4], uy_r.at[k, 0, 4])
            arrived(uall.at[k, yy(4), pl.ds(2, 2)], uy_s.at[k, 1, 4], uy_r.at[k, 1, 4])
        if step <= 3:
            h = step
            if h > 0:
                arrived(vall.at[k, yy(-h), x], vy_s.at[k, 0, h], vy_r.at[k, 0, h])
                arrived(vall.at[k, yy(h), x], vy_s.at[k, 1, h], vy_r.at[k, 1, h])
            up, down = (vall.at[k, yy(-h), x], vall.at[k, yy(h), x])
            if h == 3:
                up, down = (up.at[pl.ds(0, 32)], down.at[pl.ds(32, 32)])
            send(up, up, vy_s.at[k, 0, h + 1], vy_r.at[k, 0, h + 1], at_y(1))
            send(down, down, vy_s.at[k, 1, h + 1], vy_r.at[k, 1, h + 1], at_y(NY - 1))
        if step == 4:
            arrived(vall.at[k, yy(4), x, pl.ds(0, 32)], vy_s.at[k, 0, 4], vy_r.at[k, 0, 4])
            arrived(vall.at[k, yy(4), x, pl.ds(32, 32)], vy_s.at[k, 1, 4], vy_r.at[k, 1, 4])
            for dx in range(1, NX):
                send(vall.at[k, :, x], vall.at[k, :, x], vx_s.at[k, dx], vx_r.at[k, dx], at_x(dx))
        if step == 5:
            for dx in range(1, NX):
                arrived(vall.at[k, :, lax.rem(x + NX - dx, NX)], vx_s.at[k, dx], vx_r.at[k, dx])

    todo = sorted(((2 * k + step, k, step) for k in range(WIN) for step in range(6)))
    done = set()

    def pump(count):
        for _ in range(min(count, len(todo))):
            _, k, step = todo.pop(0)
            gather_step(k, step)
            done.add((k, step))

    def pump_through(k):
        while (k, 5) not in done:
            pump(1)

    def gather_pieces(pieces, a):
        for dz in FAR_FIRST:
            send(pieces.at[p], pieces.at[p], ag_s.at[a, dz], ag_r.at[a, dz], at_z(dz, c))
        send(pieces.at[p], pieces.at[p], fw_s.at[a, 0], fw_r.at[a, 0], at_z(0, 1 - c))
        pump(2)
        for dz in NEAR_FIRST:
            piece = pieces.at[lax.rem(z + NZ - dz, NZ) * 2 + c]
            arrived(piece, ag_s.at[a, dz], ag_r.at[a, dz])
            send(piece, piece, fw_s.at[a, dz], fw_r.at[a, dz], at_z(0, 1 - c))
        for dz in range(NZ):
            piece = pieces.at[lax.rem(z + NZ - dz, NZ) * 2 + 1 - c]
            arrived(piece, fw_s.at[a, dz], fw_r.at[a, dz])

    stored = [owners[i] for i in range(16)]
    my_row = stored[0]
    for i in range(1, 16):
        my_row = jnp.where(p == i, stored[i], my_row)

    gather_step(0, 0)
    todo.pop(0)
    for g in range(NY):
        rows = rhs[0, pl.ds(256 * g, 256), :]
        stage[0, g] = rows.reshape(2, 128, 128)
        res[pl.ds(256 * g, 256), :] = rows.astype(jnp.float32)

    for j in range(WIN):
        mine = jnp.full((128, 128), my_row, jnp.int32) == j
        send(stage.at[j, :, 1 - c], sibb.at[j], sib_s.at[j], sib_r.at[j], at_z(0, 1 - c))
        pump(1)
        arrived(sibb.at[j], sib_s.at[j], sib_r.at[j])
        sib_row = stored[0]
        for i in range(1, 16):
            sib_row = jnp.where(p + 1 - 2 * c == i, stored[i], sib_row)
        sibs = jnp.full((128, 128), sib_row, jnp.int32) == j
        zero = jnp.zeros((128, 128), jnp.float32)
        for g in range(NZ):
            own = jnp.where(mine, stage[j, g, c].astype(jnp.float32), zero)
            other = jnp.where(sibs, sibb[j, g].astype(jnp.float32), own)
            comb[j, g] = other.astype(jnp.bfloat16)
        for dz in FAR_FIRST:
            send(comb.at[j, lax.rem(z + dz, NZ)], rsb.at[j, dz], rs_s.at[j, dz], rs_r.at[j, dz], at_z(dz, c))
        pump(1)
        total = comb[j, z].astype(jnp.float32)
        for dz in NEAR_FIRST:
            arrived(rsb.at[j, dz], rs_s.at[j, dz], rs_r.at[j, dz])
            total = total + rsb[j, dz].astype(jnp.float32)
        nag[j, p] = total.astype(jnp.bfloat16)
        gather_pieces(nag.at[j], 2 * j)
        acc = jnp.zeros((128, 128), jnp.float32)
        for g in range(NZ):
            acc += jnp.dot(
                d[j, :, pl.ds(256 * g, 256)], nag[j, pl.ds(2 * g, 2)].reshape(256, 128),
                preferred_element_type=jnp.float32,
            )
        solved[j] = acc.astype(jnp.bfloat16)
        xag[j, p] = acc.T.astype(jnp.bfloat16)
        gather_pieces(xag.at[j], 2 * j + 1)
        pump_through(j)
        ct = jnp.zeros((128, 256), jnp.float32)
        for g in range(NY):
            both = jnp.concatenate([xag[j, 2 * g], xag[j, 2 * g + 1]], axis=1)
            ct += jnp.dot(both, vall[j, g].reshape(256, 256), preferred_element_type=jnp.float32)
        keep = lax.broadcasted_iota(jnp.int32, (128, 256), 1) < jnp.where(j < my_row, ranks[0, j], 0)
        coeffs = jnp.where(keep, ct, 0.0).T.astype(jnp.bfloat16)
        for g in range(NY):
            rows = pl.ds(256 * g, 256)
            new = res[rows, :] - jnp.dot(
                uall[j, g].reshape(256, 256), coeffs, preferred_element_type=jnp.float32
            )
            if j < WIN - 1:
                res[rows, :] = new
                stage[j + 1, g] = new.astype(jnp.bfloat16).reshape(2, 128, 128)
            else:
                updated[0, rows, :] = new.astype(jnp.bfloat16)
    for copy in sent:
        copy.wait_send()


def body(rhs_blocks, left_u, left_v, tile_ranks, diag_inverse, row_owner):
    vmem, smem = (pl.BlockSpec(memory_space=pltpu.VMEM), pl.BlockSpec(memory_space=pltpu.SMEM))
    bf16 = jnp.bfloat16
    dma = pltpu.SemaphoreType.DMA
    return tuple(pl.pallas_call(
        kernel,
        out_shape=(
            jax.ShapeDtypeStruct((WIN, 128, 128), bf16),
            jax.ShapeDtypeStruct((1, 2048, 128), bf16),
        ),
        in_specs=[smem, smem, vmem, vmem, vmem, vmem],
        out_specs=(vmem, vmem),
        scratch_shapes=[
            pltpu.VMEM((WIN, NY, NX, 64, 256), bf16),
            pltpu.VMEM((WIN, NY, NX, 64, 256), bf16),
            pltpu.VMEM((2048, 128), jnp.float32),
            pltpu.VMEM((WIN, NZ, 2, 128, 128), bf16),
            pltpu.VMEM((WIN, NZ, 128, 128), bf16),
            pltpu.VMEM((WIN, NZ, 128, 128), bf16),
            pltpu.VMEM((WIN, NZ, 128, 128), bf16),
            pltpu.VMEM((WIN, 16, 128, 128), bf16),
            pltpu.VMEM((WIN, 16, 128, 128), bf16),
            dma((WIN, 4)), dma((WIN, 4)),
            dma((WIN, 2, 5)), dma((WIN, 2, 5)),
            dma((WIN, 2, 5)), dma((WIN, 2, 5)),
            dma((WIN, 4)), dma((WIN, 4)),
            dma((WIN,)), dma((WIN,)),
            dma((WIN, 8)), dma((WIN, 8)),
            dma((2 * WIN, 8)), dma((2 * WIN, 8)),
            dma((2 * WIN, 8)), dma((2 * WIN, 8)),
        ],
        compiler_params=pltpu.CompilerParams(
            collective_id=0, has_side_effects=True, vmem_limit_bytes=48 << 20
        ),
        name="substitution",
    )(tile_ranks, row_owner, rhs_blocks, left_u, left_v, diag_inverse))


def solution(mesh):
    return jax.shard_map(
        body,
        mesh=mesh,
        in_specs=(
            P("rows", None, "rhs"),
            P("rows", None, "rhs", None),
            P("rows", None, "rhs", None),
            P("rows", None),
            P(None, "rows", None),
            P(),
        ),
        out_specs=(P(None, "rows", "rhs"), P("rows", None, "rhs")),
        check_vma=False,
    )
```

```python
import jax
import jax.numpy as jnp
from jax import lax
from jax.experimental import pallas as pl
from jax.experimental.pallas import tpu as pltpu
from jax.sharding import PartitionSpec as P

MESH = pl.DeviceIdType.MESH
NZ, NY, NX, WIN = 8, 8, 4, 4
NEAR = WIN - 1
FAR_FIRST = (4, 3, 5, 2, 6, 1, 7)
NEAR_FIRST = (1, 7, 2, 6, 3, 5, 4)
F32, BF16 = jnp.float32, jnp.bfloat16
BEGIN = {0: 0, 4: 2.5, 1: 5, 5: 6.5, 2: 9, 6: 10.5, 3: 12}


def dot(a, b):
    return jnp.dot(a, b, preferred_element_type=F32)


def kernel(ranks, owners, rhs, u, v, d, solved, updated, uall, vall, cu, cv, uown, vown, rin, dchip, res, stage,
           sibb, comb, rsb, nag, xag, cmine, cout, csib, ccomb, crs, cown, ysend, yrecv, lsem, ssem, rsem):
    p, q = lax.axis_index("rows"), lax.axis_index("rhs")
    z, c, y, x = p // 2, p % 2, q // 4, q % 4

    loads = []
    for i, (src, dst) in enumerate(
        ((u.at[0], uown), (v.at[0], vown), (rhs, rin), (d, dchip.at[:, pl.ds(0, 128)]))
    ):
        load = pltpu.make_async_copy(src, dst, lsem.at[i])
        load.start()
        loads.append(load)

    def at_z(dz, core):
        return {"rows": lax.rem(z + dz, NZ) * 2 + core, "rhs": q}

    def at_y(dy):
        return {"rows": p, "rhs": lax.rem(y + dy, NY) * 4 + x}

    def at_x(dx):
        return {"rows": p, "rhs": y * 4 + lax.rem(x + dx, NX)}

    sib = at_z(0, 1 - c)
    barrier = pltpu.get_barrier_semaphore()
    peers = [sib] + [at_z(dz, c) for dz in range(1, NZ)]
    peers += [at_y(1), at_y(NY - 1)] + [at_x(dx) for dx in range(1, NX)]
    for peer in peers:
        pl.semaphore_signal(barrier, inc=1, device_id=peer, device_id_type=MESH)

    numbers, sent = {}, []

    def copy_of(key, src, dst, peer):
        n = numbers.setdefault(key, len(numbers))
        return pltpu.make_async_remote_copy(
            src_ref=src, dst_ref=dst, send_sem=ssem.at[n], recv_sem=rsem.at[n], device_id=peer, device_id_type=MESH
        )

    def send(key, src, dst, peer):
        copy = copy_of(key, src, dst, peer)
        copy.start()
        sent.append(copy)

    def arrived(key, dst):
        copy_of(key, dst, dst, sib).wait_recv()

    def zz(dz):
        return lax.rem(z + NZ - dz, NZ)

    def yy(dy):
        return lax.rem(y + dy + NY, NY)

    def xx(dx):
        return lax.rem(x + NX - dx, NX)

    def gather_step(e, step):
        if e < WIN:
            ub, vb, ua, va = uown.at[e], vown.at[e], uall.at[e], vall.at[e]
        else:
            t = e - WIN
            ub, vb, ua, va = cown.at[0, t], cown.at[1, t], cu.at[t], cv.at[t]
        if step == 0:
            for dx in range(1, NX):
                send(("ux", e, dx), ub, ua.at[y, x], at_x(dx))
            ua[y, x] = ub[...]
            va[y, x] = vb[...]
        if step == 1:
            for dx in range(1, NX):
                arrived(("ux", e, dx), ua.at[y, xx(dx)])
        if 1 <= step <= 4:
            h = step - 1
            if h > 0:
                arrived(("uy+", e, h), ua.at[yy(-h)])
                arrived(("uy-", e, h), ua.at[yy(h)])
            up, down = (ua.at[yy(-h)], ua.at[yy(h)])
            if h == 3:
                up, down = (up.at[pl.ds(0, 2)], down.at[pl.ds(2, 2)])
            send(("uy+", e, h + 1), up, up, at_y(1))
            send(("uy-", e, h + 1), down, down, at_y(NY - 1))
        if step == 5:
            arrived(("uy+", e, 4), ua.at[yy(4), pl.ds(0, 2)])
            arrived(("uy-", e, 4), ua.at[yy(4), pl.ds(2, 2)])
        if step <= 3:
            h = step
            if h > 0:
                arrived(("vy+", e, h), va.at[yy(-h), x])
                arrived(("vy-", e, h), va.at[yy(h), x])
            up, down = (va.at[yy(-h), x], va.at[yy(h), x])
            if h == 3:
                up, down = (up.at[pl.ds(0, 32)], down.at[pl.ds(32, 32)])
            send(("vy+", e, h + 1), up, up, at_y(1))
            send(("vy-", e, h + 1), down, down, at_y(NY - 1))
        if step == 4:
            arrived(("vy+", e, 4), va.at[yy(4), x, pl.ds(0, 32)])
            arrived(("vy-", e, 4), va.at[yy(4), x, pl.ds(32, 32)])
            for dx in range(1, NX):
                send(("vx", e, dx), va.at[:, x], va.at[:, x], at_x(dx))
        if step == 5:
            for dx in range(1, NX):
                arrived(("vx", e, dx), va.at[:, xx(dx)])

    todo = sorted((b + step, e, step) for e, b in BEGIN.items() for step in range(6))
    done = set()

    def pump(count):
        for _ in range(min(count, len(todo))):
            _, e, step = todo.pop(0)
            gather_step(e, step)
            done.add((e, step))

    def pump_through(e):
        while (e, 5) not in done:
            pump(1)

    def ag_send(pieces, a):
        for dz in FAR_FIRST:
            send((a, dz), pieces.at[p], pieces.at[p], at_z(dz, c))
        send((a, "f", 0), pieces.at[p], pieces.at[p], sib)

    def ag_forward(pieces, a):
        for dz in NEAR_FIRST:
            piece = pieces.at[zz(dz) * 2 + c]
            arrived((a, dz), piece)
            send((a, "f", dz), piece, piece, sib)

    def ag_finish(pieces, a):
        for dz in range(NZ):
            arrived((a, "f", dz), pieces.at[zz(dz) * 2 + 1 - c])

    stored = [owners[i] for i in range(16)]
    my_row, sib_row = stored[0], stored[0]
    for i in range(1, 16):
        my_row = jnp.where(p == i, stored[i], my_row)
        sib_row = jnp.where(p + 1 - 2 * c == i, stored[i], sib_row)

    def is_row(row, j, shape):
        return jnp.full(shape, row, jnp.int32) == j

    def scatter(j, own, other):
        square = (128, 128)
        mine, sibs = is_row(my_row, j, square), is_row(sib_row, j, square)
        zero = jnp.zeros(square, F32)
        for g in range(NZ):
            far = jnp.where(sibs, other[g].astype(F32), zero)
            comb[j, g] = jnp.where(mine, own[g, c].astype(F32), far).astype(BF16)
        for dz in FAR_FIRST:
            send(("rs", j, dz), comb.at[j, lax.rem(z + dz, NZ)], rsb.at[j, dz], at_z(dz, c))

    def scattered(j):
        total = comb[j, z].astype(F32)
        for dz in NEAR_FIRST:
            arrived(("rs", j, dz), rsb.at[j, dz])
            total = total + rsb[j, dz].astype(F32)
        nag[j, p] = total.astype(BF16)
        ag_send(nag.at[j], ("n", j))

    def solve_far(j):
        acc = jnp.zeros((128, 128), F32)
        for g in range(NZ):
            acc += dot(dchip[j, pl.ds(0, 128), pl.ds(256 * g, 256)], nag[j, pl.ds(2 * g, 2)].reshape(256, 128))
        return acc

    def store_solved(j, value):
        solved[j] = value.astype(BF16)
        xag[j, p] = value.T.astype(BF16)
        ag_send(xag.at[j], ("x", j))

    def times_solved(j, factor):
        total = None
        for g in range(NY):
            both = jnp.concatenate([xag[j, 2 * g], xag[j, 2 * g + 1]], axis=1)
            term = dot(both, factor(g))
            total = term if total is None else total + term
        return total

    def near_term(t):
        coeffs = times_solved(t, lambda g: cv[t, g].reshape(256, 128)).T.astype(BF16)
        total = jnp.zeros((256, 128), F32)
        for g in range(NY):
            part = dot(cu[t, g].reshape(256, 128), coeffs).astype(BF16)
            total += dot(dchip[t + 1, :, pl.ds(256 * g, 256)], part)
        ysend[t] = total[128:]
        send(("y", t), ysend.at[t], yrecv.at[t], sib)
        return total[:128]

    def update(k):
        ct = times_solved(k, lambda g: vall[k, g].reshape(256, 256))
        keep = lax.broadcasted_iota(jnp.int32, (128, 256), 1) < jnp.where(k < my_row, ranks[0, k], 0)
        coeffs = jnp.where(keep, ct, 0.0).T.astype(BF16)
        for g in range(NY):
            old = rin[g].reshape(256, 128).astype(F32) if k == 0 else res[g]
            new = old - dot(uall[k, g].reshape(256, 256), coeffs)
            if k < WIN - 1:
                res[g] = new
            if k < WIN - 2:
                stage[k, g] = new.astype(BF16).reshape(2, 128, 128)
            if k == WIN - 1:
                updated[g] = new.astype(BF16).reshape(2, 128, 128)

    for load in loads[:3]:
        load.wait()
    for t in range(NEAR):
        half = (64, 128)
        mine = is_row(my_row, t + 1, half)
        left = is_row(c, 0, half)
        lane = lax.broadcasted_iota(jnp.int32, half, 1)
        for i, own in enumerate((uown, vown)):
            a, b = own[t, :, :128].astype(F32), own[t, :, 128:].astype(F32)
            a, b = jnp.where(mine, a, 0.0), jnp.where(mine, b, 0.0)
            if i == 1:
                a, b = jnp.where(lane < ranks[0, t], a, 0.0), jnp.where(lane + 128 < ranks[0, t], b, 0.0)
            cmine[i, t] = jnp.where(left, a, b)
            cout[i, t] = jnp.where(left, b, a).astype(BF16)

    pl.semaphore_wait(barrier, len(peers))
    send(("r", 0), rin.at[:, 1 - c], sibb.at[0], sib)
    send(("c",), cout, csib, sib)
    pump(1)
    arrived(("r", 0), sibb.at[0])
    scatter(0, rin, sibb.at[0])
    arrived(("c",), csib)
    for i in range(NZ):
        rows = pl.ds(16 * (i % 4), 16)
        ccomb[i] = (cmine[i // 4, :, rows] + csib[i // 4, :, rows].astype(F32)).astype(BF16)
    for dz in FAR_FIRST:
        send(("crs", dz), ccomb.at[lax.rem(z + dz, NZ)], crs.at[dz], at_z(dz, c))
    loads[3].wait()
    ownd = dchip.at[pl.ds(1, NEAR), pl.ds(0, 128)]
    send(("d",), ownd, dchip.at[pl.ds(1, NEAR), pl.ds(128, 128)], sib)
    pump(1)
    scattered(0)
    total = ccomb[z].astype(F32)
    for dz in NEAR_FIRST:
        arrived(("crs", dz), crs.at[dz])
        total = total + crs[dz].astype(F32)
    place = cown.at[z // 4, :, pl.ds(pl.multiple_of(16 * (z % 4), 16), 16)]
    place[...] = total.astype(BF16)
    for dz in FAR_FIRST:
        send(("cag", dz), place, place, at_z(dz, c))
    scatter(1, rin, sibb.at[0])
    pump(1)
    ag_forward(nag.at[0], ("n", 0))
    for dz in NEAR_FIRST:
        arrived(("cag", dz), cown.at[zz(dz) // 4, :, pl.ds(pl.multiple_of(16 * (zz(dz) % 4), 16), 16)])
    pump(1)
    ag_finish(nag.at[0], ("n", 0))
    store_solved(0, solve_far(0))
    pump(3)
    scattered(1)
    pump(3)
    arrived(("d",), dchip.at[pl.ds(1, NEAR), pl.ds(128, 128)])
    for j in range(WIN):
        ag_forward(xag.at[j], ("x", j))
        if j in (1, 2):
            scattered(j + 1)
        ag_finish(xag.at[j], ("x", j))
        if j < WIN - 1:
            pump_through(WIN + j)
            mine = near_term(j)
            ag_forward(nag.at[j + 1], ("n", j + 1))
            pump(1)
            ag_finish(nag.at[j + 1], ("n", j + 1))
            base = solve_far(j + 1) - mine
            arrived(("y", j), yrecv.at[j])
            store_solved(j + 1, base - yrecv[j])
        pump_through(j)
        update(j)
        if j < 2:
            send(("r", j + 1), stage.at[j, :, 1 - c], sibb.at[j + 1], sib)
            pump(2)
            arrived(("r", j + 1), sibb.at[j + 1])
            scatter(j + 2, stage.at[j], sibb.at[j + 1])
        pump(5)
    for copy in sent:
        copy.wait_send()


def body(rhs_blocks, left_u, left_v, tile_ranks, diag_inverse, row_owner):
    vmem, smem, hbm = (pl.BlockSpec(memory_space=s) for s in (pltpu.VMEM, pltpu.SMEM, pl.ANY))
    blocks = (NZ, 2, 128, 128)
    solved, updated = pl.pallas_call(
        kernel,
        out_shape=(jax.ShapeDtypeStruct((WIN, 128, 128), BF16), jax.ShapeDtypeStruct(blocks, BF16)),
        in_specs=[smem, smem, hbm, hbm, hbm, hbm],
        out_specs=(vmem, vmem),
        scratch_shapes=[
            pltpu.VMEM((WIN, NY, NX, 64, 256), BF16),
            pltpu.VMEM((WIN, NY, NX, 64, 256), BF16),
            pltpu.VMEM((NEAR, NY, NX, 64, 128), BF16),
            pltpu.VMEM((NEAR, NY, NX, 64, 128), BF16),
            pltpu.VMEM((WIN, 64, 256), BF16),
            pltpu.VMEM((WIN, 64, 256), BF16),
            pltpu.VMEM(blocks, BF16),
            pltpu.VMEM((WIN, 256, 2048), BF16),
            pltpu.VMEM((NZ, 256, 128), F32),
            pltpu.VMEM((2, *blocks), BF16),
            pltpu.VMEM((3, NZ, 128, 128), BF16),
            pltpu.VMEM((WIN, NZ, 128, 128), BF16),
            pltpu.VMEM((WIN, NZ, 128, 128), BF16),
            pltpu.VMEM((WIN, 16, 128, 128), BF16),
            pltpu.VMEM((WIN, 16, 128, 128), BF16),
            pltpu.VMEM((2, NEAR, 64, 128), F32),
            pltpu.VMEM((2, NEAR, 64, 128), BF16),
            pltpu.VMEM((2, NEAR, 64, 128), BF16),
            pltpu.VMEM((NZ, NEAR, 16, 128), BF16),
            pltpu.VMEM((NZ, NEAR, 16, 128), BF16),
            pltpu.VMEM((2, NEAR, 64, 128), BF16),
            pltpu.VMEM((NEAR, 128, 128), F32),
            pltpu.VMEM((NEAR, 128, 128), F32),
            pltpu.SemaphoreType.DMA((4,)),
            pltpu.SemaphoreType.DMA((400,)),
            pltpu.SemaphoreType.DMA((400,)),
        ],
        compiler_params=pltpu.CompilerParams(
            collective_id=0, has_side_effects=True, vmem_limit_bytes=48 << 20
        ),
        name="substitution",
    )(tile_ranks, row_owner, rhs_blocks.reshape(blocks), left_u, left_v, diag_inverse)
    return solved, updated.reshape(1, 2048, 128)


def solution(mesh):
    return jax.shard_map(
        body,
        mesh=mesh,
        in_specs=(
            P("rows", None, "rhs"),
            P("rows", None, "rhs", None),
            P("rows", None, "rhs", None),
            P("rows", None),
            P(None, "rows", None),
            P(),
        ),
        out_specs=(P(None, "rows", "rhs"), P("rows", None, "rhs")),
        check_vma=False,
    )
```

```python
import jax
import jax.numpy as jnp
from jax import lax
from jax.experimental import pallas as pl
from jax.experimental.pallas import tpu as pltpu
from jax.sharding import PartitionSpec as P

MESH = pl.DeviceIdType.MESH
NZ, NY, NX, WIN = 8, 8, 4, 4
FAR_FIRST = (4, 3, 5, 2, 6, 1, 7)
NEAR_FIRST = (1, 7, 2, 6, 3, 5, 4)
PAIRS = ((1, 0), (3, 2))
F32, BF16 = jnp.float32, jnp.bfloat16
OWN = {"m0": (0, 2), "m2": (2, 2)}
ORDER = (
    "m0v0", "m0u0", "m0v1", "m0u1", "m0v2", "m0v3", "m0u2", "p1_0", "m0v4", "p1_1", "m0u3", "p1_2", "m0u4", "p1_3",
    "m0u5", "m0v5", "m0v6", "m0u6", "m2v0", "m2u0", "m2v1", "m2u1", "m2v2", "m2v3", "m2u2", "p3_0", "m2v4", "m2u3",
    "p3_1", "m2u4", "p3_2", "m2v5", "p3_3", "m2u5", "m2v6", "m2u6",
)


def dot(a, b):
    return jnp.dot(a, b, preferred_element_type=F32)


def kernel(ranks, owners, rhs, u, v, d, solved, updated, uall, vall, cuv, uown, vown, rin, dchip, res,
           stage, sibb, comb, rsb, nag, xag, cout, crs, cown, ysend, yrecv, lsem, ssem, rsem):
    p, q = lax.axis_index("rows"), lax.axis_index("rhs")
    z, c, y, x = p // 2, p % 2, q // 4, q % 4

    loads = []
    for i, (src, dst) in enumerate(
        ((u.at[0], uown), (v.at[0], vown), (rhs, rin), (d, dchip.at[:, pl.ds(0, 128)]))
    ):
        load = pltpu.make_async_copy(src, dst, lsem.at[i])
        load.start()
        loads.append(load)

    def at_z(dz, core):
        return {"rows": lax.rem(z + dz, NZ) * 2 + core, "rhs": q}

    def at_y(dy):
        return {"rows": p, "rhs": lax.rem(y + dy, NY) * 4 + x}

    def at_x(dx):
        return {"rows": p, "rhs": y * 4 + lax.rem(x + dx, NX)}

    sib = at_z(0, 1 - c)
    ring = [(dz, core) for dz in FAR_FIRST for core in (c, 1 - c)] + [(0, 1 - c)]
    barrier = pltpu.get_barrier_semaphore()
    peers = [at_z(dz, core) for dz, core in ring]
    peers += [at_y(dy) for dy in range(1, NY)] + [at_x(dx) for dx in range(1, NX)]
    for peer in peers:
        pl.semaphore_signal(barrier, inc=1, device_id=peer, device_id_type=MESH)

    numbers, sent = {}, []

    def copy_of(key, src, dst, peer):
        n = numbers.setdefault(key, len(numbers))
        return pltpu.make_async_remote_copy(
            src_ref=src, dst_ref=dst, send_sem=ssem.at[n], recv_sem=rsem.at[n], device_id=peer, device_id_type=MESH
        )

    def send(key, src, dst, peer):
        copy = copy_of(key, src, dst, peer)
        copy.start()
        sent.append(copy)

    def arrived(key, dst):
        copy_of(key, dst, dst, sib).wait_recv()

    def zz(dz):
        return lax.rem(z + NZ - dz, NZ)

    def yy(dy):
        return lax.rem(y + dy + NY, NY)

    def xx(dx):
        return lax.rem(x + NX - dx, NX)

    def place_own(own, into):
        for i in range(own.shape[0]):
            into[i, y, x] = own[i]

    def y_first(key, own, into, step):
        if step == 0:
            place_own(own, into)
        if 1 <= step <= 4:
            arrive = [into.at[:, yy(-step), x], into.at[:, yy(step), x]]
            if step == 4:
                arrive = [arrive[0].at[:, pl.ds(0, 32)], arrive[1].at[:, pl.ds(32, 32)]]
            arrived((key, "y+", step), arrive[0])
            arrived((key, "y-", step), arrive[1])
        if step <= 3:
            up, down = (into.at[:, yy(-step), x], into.at[:, yy(step), x])
            if step == 3:
                up, down = (up.at[:, pl.ds(0, 32)], down.at[:, pl.ds(32, 32)])
            send((key, "y+", step + 1), up, up, at_y(1))
            send((key, "y-", step + 1), down, down, at_y(NY - 1))
        if step == 4:
            send((key, "x+", 1), into.at[:, :, x], into.at[:, :, x], at_x(1))
            send((key, "x-", 1), into.at[:, :, x], into.at[:, :, x], at_x(NX - 1))
        low, high = pl.ds(0, 4), pl.ds(4, 4)
        if step == 5:
            arrived((key, "x+", 1), into.at[:, :, xx(1)])
            arrived((key, "x-", 1), into.at[:, :, xx(-1)])
            send((key, "x+", 2), into.at[:, low, xx(1)], into.at[:, low, xx(1)], at_x(1))
            send((key, "x-", 2), into.at[:, high, xx(-1)], into.at[:, high, xx(-1)], at_x(NX - 1))
        if step == 6:
            arrived((key, "x+", 2), into.at[:, low, xx(2)])
            arrived((key, "x-", 2), into.at[:, high, xx(2)])

    def x_first(key, own, into, step):
        if step == 0:
            for dx in range(1, NX):
                send((key, "x", dx), own, into.at[:, y, x], at_x(dx))
            place_own(own, into)
        if step == 1:
            for dx in range(1, NX):
                arrived((key, "x", dx), into.at[:, y, xx(dx)])
        h = step - 1
        if 1 <= h <= 4:
            arrive = [into.at[:, yy(-h)], into.at[:, yy(h)]]
            if h == 4:
                arrive = [arrive[0].at[:, pl.ds(0, 2)], arrive[1].at[:, pl.ds(2, 2)]]
            arrived((key, "y+", h), arrive[0])
            arrived((key, "y-", h), arrive[1])
        if 0 <= h <= 3:
            up, down = (into.at[:, yy(-h)], into.at[:, yy(h)])
            if h == 3:
                up, down = (up.at[:, pl.ds(0, 2)], down.at[:, pl.ds(2, 2)])
            send((key, "y+", h + 1), up, up, at_y(1))
            send((key, "y-", h + 1), down, down, at_y(NY - 1))

    def pair_step(t, step):
        into, low, high = cuv.at[:, t], pl.ds(0, 4), pl.ds(4, 4)
        if step == 0:
            for dy in FAR_FIRST:
                send(("py", t, dy), cown.at[:, t], into.at[:, y, x], at_y(dy))
            for i in range(2):
                cuv[i, t, y, x] = cown[i, t]
        if step == 1:
            for dy in NEAR_FIRST:
                arrived(("py", t, dy), into.at[:, yy(-dy), x])
            send(("px+", t, 1), into.at[:, :, x], into.at[:, :, x], at_x(1))
            send(("px-", t, 1), into.at[:, :, x], into.at[:, :, x], at_x(NX - 1))
        if step == 2:
            arrived(("px+", t, 1), into.at[:, :, xx(1)])
            arrived(("px-", t, 1), into.at[:, :, xx(-1)])
            send(("px+", t, 2), into.at[:, low, xx(1)], into.at[:, low, xx(1)], at_x(1))
            send(("px-", t, 2), into.at[:, high, xx(-1)], into.at[:, high, xx(-1)], at_x(NX - 1))
        if step == 3:
            arrived(("px+", t, 2), into.at[:, low, xx(2)])
            arrived(("px-", t, 2), into.at[:, high, xx(2)])

    def take(name, part, step):
        if name == "p1" or name == "p3":
            pair_step(int(name[1]) // 2, step)
        else:
            i, first = (0, x_first) if part == "u" else (1, y_first)
            group = pl.ds(*OWN[name])
            first((name, part), (uown, vown)[i].at[group], (uall, vall)[i].at[group], step)

    todo = list(ORDER)
    done = set()

    def pump(count):
        for _ in range(min(count, len(todo))):
            item = todo.pop(0)
            take(item[:2], item[2], int(item[3]))
            done.add(item)

    def pump_through(name):
        last = {name + "_3"} if name[0] == "p" else {name + "u6", name + "v6"}
        while not last <= done:
            pump(1)

    def ag_send(pieces, a):
        for dz in FAR_FIRST:
            send((a, dz), pieces.at[p], pieces.at[p], at_z(dz, c))
        send((a, "f", 0), pieces.at[p], pieces.at[p], sib)

    def ag_forward(pieces, a):
        for dz in NEAR_FIRST:
            piece = pieces.at[zz(dz) * 2 + c]
            arrived((a, dz), piece)
            send((a, "f", dz), piece, piece, sib)

    def ag_finish(pieces, a):
        for dz in range(NZ):
            arrived((a, "f", dz), pieces.at[zz(dz) * 2 + 1 - c])

    stored = [owners[i] for i in range(16)]
    my_row, sib_row = stored[0], stored[0]
    holder = [jnp.int32(0) for _ in range(WIN)]
    for i in range(16):
        my_row = jnp.where(p == i, stored[i], my_row)
        sib_row = jnp.where(p + 1 - 2 * c == i, stored[i], sib_row)
        holder = [jnp.where(stored[i] == j, i, h) for j, h in enumerate(holder)]

    def scatter(j, own, other):
        square = (128, 128)
        mine = jnp.full(square, my_row, jnp.int32) == j
        sibs = jnp.full(square, sib_row, jnp.int32) == j
        for g in range(NZ):
            far = jnp.where(sibs, other[g].astype(F32), 0.0)
            comb[j, g] = jnp.where(mine, own[g, c].astype(F32), far).astype(BF16)
        for dz in FAR_FIRST:
            send(("rs", j, dz), comb.at[j, lax.rem(z + dz, NZ)], rsb.at[j, dz], at_z(dz, c))

    def scattered(j):
        total = comb[j, z].astype(F32)
        for dz in NEAR_FIRST:
            arrived(("rs", j, dz), rsb.at[j, dz])
            total = total + rsb[j, dz].astype(F32)
        nag[j, p] = total.astype(BF16)

    def solve_far(j):
        acc = jnp.zeros((128, 128), F32)
        for g in range(NZ):
            acc += dot(dchip[j, pl.ds(0, 128), pl.ds(256 * g, 256)], nag[j, pl.ds(2 * g, 2)].reshape(256, 128))
        return acc

    def store_solved(j, value):
        solved[j] = value.astype(BF16)
        xag[j, p] = value.T.astype(BF16)
        ag_send(xag.at[j], ("x", j))

    def times_solved(j, factor):
        total = None
        for g in range(NY):
            both = jnp.concatenate([xag[j, 2 * g], xag[j, 2 * g + 1]], axis=1)
            term = dot(both, factor(g))
            total = term if total is None else total + term
        return total

    def pair_term(j, k):
        t = PAIRS.index((j, k))
        coeffs = times_solved(k, lambda g: cuv[1, t, g].reshape(256, 128)).T.astype(BF16)
        total = jnp.zeros((256, 128), F32)
        for g in range(NY):
            part = dot(cuv[0, t, g].reshape(256, 128), coeffs).astype(BF16)
            total += dot(dchip[j, :, pl.ds(256 * g, 256)], part)
        return total

    def update(k):
        ct = times_solved(k, lambda g: vall[k, g].reshape(256, 256))
        keep = lax.broadcasted_iota(jnp.int32, (128, 256), 1) < jnp.where(k < my_row, ranks[0, k], 0)
        coeffs = jnp.where(keep, ct, 0.0).T.astype(BF16)
        for g in range(NY):
            old = rin[g].reshape(256, 128).astype(F32) if k == 0 else res[g]
            new = old - dot(uall[k, g].reshape(256, 256), coeffs)
            if k < WIN - 1:
                res[g] = new
            if k == 1:
                stage[g] = new.astype(BF16).reshape(2, 128, 128)
            if k == WIN - 1:
                updated[g] = new.astype(BF16).reshape(2, 128, 128)

    for load in loads[:3]:
        load.wait()
    lane = lax.broadcasted_iota(jnp.int32, (64, 128), 1)
    for t, (_, k) in enumerate(PAIRS):
        for core in range(2):
            lanes = pl.ds(128 * core, 128)
            us = uown[k, :, lanes].reshape(4, 16, 128)
            vs = vown[k, :, lanes].astype(F32)
            vs = jnp.where(lane + 128 * core < ranks[0, k], vs, 0.0).astype(BF16).reshape(4, 16, 128)
            for i in range(4):
                cout[2 * i + core, t] = us[i]
                cout[8 + 2 * i + core, t] = vs[i]

    pl.semaphore_wait(barrier, len(peers))
    send(("r", 0), rin.at[:, 1 - c], sibb.at[0], sib)
    for i, (dz, core) in enumerate(ring):
        to = lax.rem(z + dz, NZ) * 2 + core
        send(("c", i), cout.at[to], crs.at[p], at_z(dz, core))
    pump(2)
    crs[p] = cout[p]
    arrived(("r", 0), sibb.at[0])
    scatter(0, rin, sibb.at[0])
    scatter(1, rin, sibb.at[0])
    loads[3].wait()
    near_d = [dchip.at[j, pl.ds(0, 128)] for j, _ in PAIRS]
    far_d = [dchip.at[j, pl.ds(128, 128)] for j, _ in PAIRS]
    for t in range(len(PAIRS)):
        send(("d", t), near_d[t], far_d[t], sib)
    pump(2)
    for i, (dz, core) in enumerate(ring):
        arrived(("c", i), crs.at[zz(dz) * 2 + core])
    part = pl.ds(pl.multiple_of(16 * (z % 4), 16), 16)
    for t, (j, _) in enumerate(PAIRS):
        cown[z // 4, t, part] = crs[holder[j], t]
    for dz in FAR_FIRST:
        place = cown.at[z // 4, :, part]
        send(("cag", dz), place, place, at_z(dz, c))
    pump(1)
    scattered(0)
    ag_send(nag.at[0], "n0")
    pump(2)
    for dz in NEAR_FIRST:
        arrived(("cag", dz), cown.at[zz(dz) // 4, :, pl.ds(pl.multiple_of(16 * (zz(dz) % 4), 16), 16)])
    pump(2)
    scattered(1)
    ag_forward(nag.at[0], "n0")
    ag_finish(nag.at[0], "n0")
    for j in range(WIN):
        even = j % 2 == 0
        if even:
            store_solved(j, solve_far(j))
            ag_send(nag.at[j + 1], "n" + str(j + 1))
        pump((2, 4, 4, 0)[j])
        ag_forward(xag.at[j], ("x", j))
        pump((1, 0, 0, 0)[j])
        ag_finish(xag.at[j], ("x", j))
        if even:
            t = j // 2
            pump_through("p" + str(j + 1))
            arrived(("d", t), far_d[t])
            term = pair_term(j + 1, j)
            ysend[t] = term[128:]
            send(("y", t), ysend.at[t], yrecv.at[t], sib)
            ag_forward(nag.at[j + 1], "n" + str(j + 1))
            ag_finish(nag.at[j + 1], "n" + str(j + 1))
            known = solve_far(j + 1) - term[:128]
            arrived(("y", t), yrecv.at[t])
            store_solved(j + 1, known - yrecv[t])
            pump_through("m" + str(j))
        update(j)
        if j == 1:
            send(("r", 1), stage.at[:, 1 - c], sibb.at[1], sib)
            arrived(("r", 1), sibb.at[1])
            scatter(2, stage, sibb.at[1])
            scatter(3, stage, sibb.at[1])
            pump(3)
            scattered(2)
            ag_send(nag.at[2], "n2")
            pump(3)
            scattered(3)
            ag_forward(nag.at[2], "n2")
            ag_finish(nag.at[2], "n2")
    for copy in sent:
        copy.wait_send()


def body(rhs_blocks, left_u, left_v, tile_ranks, diag_inverse, row_owner):
    vmem, smem, hbm = (pl.BlockSpec(memory_space=s) for s in (pltpu.VMEM, pltpu.SMEM, pl.ANY))
    blocks = (NZ, 2, 128, 128)
    pairs = len(PAIRS)
    solved, updated = pl.pallas_call(
        kernel,
        out_shape=(jax.ShapeDtypeStruct((WIN, 128, 128), BF16), jax.ShapeDtypeStruct(blocks, BF16)),
        in_specs=[smem, smem, hbm, hbm, hbm, hbm],
        out_specs=(vmem, vmem),
        scratch_shapes=[
            pltpu.VMEM((WIN, NY, NX, 64, 256), BF16),
            pltpu.VMEM((WIN, NY, NX, 64, 256), BF16),
            pltpu.VMEM((2, pairs, NY, NX, 64, 128), BF16),
            pltpu.VMEM((WIN, 64, 256), BF16),
            pltpu.VMEM((WIN, 64, 256), BF16),
            pltpu.VMEM(blocks, BF16),
            pltpu.VMEM((WIN, 256, 2048), BF16),
            pltpu.VMEM((NZ, 256, 128), F32),
            pltpu.VMEM(blocks, BF16),
            pltpu.VMEM((2, NZ, 128, 128), BF16),
            pltpu.VMEM((WIN, NZ, 128, 128), BF16),
            pltpu.VMEM((WIN, NZ, 128, 128), BF16),
            pltpu.VMEM((WIN, 16, 128, 128), BF16),
            pltpu.VMEM((WIN, 16, 128, 128), BF16),
            pltpu.VMEM((16, pairs, 16, 128), BF16),
            pltpu.VMEM((16, pairs, 16, 128), BF16),
            pltpu.VMEM((2, pairs, 64, 128), BF16),
            pltpu.VMEM((pairs, 128, 128), F32),
            pltpu.VMEM((pairs, 128, 128), F32),
            pltpu.SemaphoreType.DMA((4,)),
            pltpu.SemaphoreType.DMA((400,)),
            pltpu.SemaphoreType.DMA((400,)),
        ],
        compiler_params=pltpu.CompilerParams(
            collective_id=0, has_side_effects=True, vmem_limit_bytes=62 << 20
        ),
        name="substitution",
    )(tile_ranks, row_owner, rhs_blocks.reshape(blocks), left_u, left_v, diag_inverse)
    return solved, updated.reshape(1, 2048, 128)


def solution(mesh):
    return jax.shard_map(
        body,
        mesh=mesh,
        in_specs=(
            P("rows", None, "rhs"),
            P("rows", None, "rhs", None),
            P("rows", None, "rhs", None),
            P("rows", None),
            P(None, "rows", None),
            P(),
        ),
        out_specs=(P(None, "rows", "rhs"), P("rows", None, "rhs")),
        check_vma=False,
    )
```

```python
import jax
import jax.numpy as jnp
from jax import lax
from jax.experimental import pallas as pl
from jax.experimental.pallas import tpu as pltpu
from jax.sharding import PartitionSpec as P

MESH = pl.DeviceIdType.MESH
NZ, NY, NX, WIN = 8, 8, 4, 4
FAR_FIRST = (4, 3, 5, 2, 6, 1, 7)
NEAR_FIRST = (1, 7, 2, 6, 3, 5, 4)
PAIRS = ((1, 0), (3, 2))
F32, BF16 = jnp.float32, jnp.bfloat16
OWN = {"m0": (0, 2), "m2": (2, 2)}
ORDER = (
    "m0v0", "m0u0", "m0v1", "m0u1", "m0v2", "m0v3", "m0u2", "p1_0", "m0v4", "p1_1", "m0u3", "p1_2", "m0v5", "m0u4",
    "p1_3", "m0v6", "m0u5", "m0u6", "m2v0", "m2u0", "m2v1", "m2u1", "m2v2", "m2v3", "m2u2", "p3_0", "m2v4", "m2u3",
    "p3_1", "m2v5", "m2u4", "p3_2", "m2v6", "p3_3", "m2u5", "m2u6",
)


def dot(a, b):
    return jnp.dot(a, b, preferred_element_type=F32)


def kernel(ranks, owners, rhs, u, v, d, solved, updated, uall, vall, cuv, uown, vown, rin, dchip, res,
           stage, sibb, comb, rsb, nag, xag, cout, crs, cown, ysend, yrecv, lsem, ssem, rsem):
    p, q = lax.axis_index("rows"), lax.axis_index("rhs")
    z, c, y, x = p // 2, p % 2, q // 4, q % 4

    loads = []
    for i, (src, dst) in enumerate(
        ((u.at[0], uown), (v.at[0], vown), (rhs, rin), (d, dchip.at[:, pl.ds(0, 128)]))
    ):
        load = pltpu.make_async_copy(src, dst, lsem.at[i])
        load.start()
        loads.append(load)

    def at_z(dz, core):
        return {"rows": lax.rem(z + dz, NZ) * 2 + core, "rhs": q}

    def at_y(dy):
        return {"rows": p, "rhs": lax.rem(y + dy, NY) * 4 + x}

    def at_x(dx):
        return {"rows": p, "rhs": y * 4 + lax.rem(x + dx, NX)}

    sib = at_z(0, 1 - c)
    ring = [(dz, core) for dz in FAR_FIRST for core in (c, 1 - c)] + [(0, 1 - c)]
    barrier = pltpu.get_barrier_semaphore()
    peers = [at_z(dz, core) for dz, core in ring]
    peers += [at_y(dy) for dy in range(1, NY)] + [at_x(dx) for dx in range(1, NX)]
    for peer in peers:
        pl.semaphore_signal(barrier, inc=1, device_id=peer, device_id_type=MESH)

    numbers, sent = {}, []

    def copy_of(key, src, dst, peer):
        n = numbers.setdefault(key, len(numbers))
        return pltpu.make_async_remote_copy(
            src_ref=src, dst_ref=dst, send_sem=ssem.at[n], recv_sem=rsem.at[n], device_id=peer, device_id_type=MESH
        )

    def send(key, src, dst, peer):
        copy = copy_of(key, src, dst, peer)
        copy.start()
        sent.append(copy)

    def arrived(key, dst):
        copy_of(key, dst, dst, sib).wait_recv()

    def zz(dz):
        return lax.rem(z + NZ - dz, NZ)

    def yy(dy):
        return lax.rem(y + dy + NY, NY)

    def xx(dx):
        return lax.rem(x + NX - dx, NX)

    def place_own(own, into):
        for i in range(own.shape[0]):
            into[i, y, x] = own[i]

    def y_first(key, own, into, step):
        if step == 0:
            place_own(own, into)
        if 1 <= step <= 4:
            arrive = [into.at[:, yy(-step), x], into.at[:, yy(step), x]]
            if step == 4:
                arrive = [arrive[0].at[:, pl.ds(0, 32)], arrive[1].at[:, pl.ds(32, 32)]]
            arrived((key, "y+", step), arrive[0])
            arrived((key, "y-", step), arrive[1])
        if step <= 3:
            up, down = (into.at[:, yy(-step), x], into.at[:, yy(step), x])
            if step == 3:
                up, down = (up.at[:, pl.ds(0, 32)], down.at[:, pl.ds(32, 32)])
            send((key, "y+", step + 1), up, up, at_y(1))
            send((key, "y-", step + 1), down, down, at_y(NY - 1))
        if step == 4:
            send((key, "x+", 1), into.at[:, :, x], into.at[:, :, x], at_x(1))
            send((key, "x-", 1), into.at[:, :, x], into.at[:, :, x], at_x(NX - 1))
        low, high = pl.ds(0, 4), pl.ds(4, 4)
        if step == 5:
            arrived((key, "x+", 1), into.at[:, :, xx(1)])
            arrived((key, "x-", 1), into.at[:, :, xx(-1)])
            send((key, "x+", 2), into.at[:, low, xx(1)], into.at[:, low, xx(1)], at_x(1))
            send((key, "x-", 2), into.at[:, high, xx(-1)], into.at[:, high, xx(-1)], at_x(NX - 1))
        if step == 6:
            arrived((key, "x+", 2), into.at[:, low, xx(2)])
            arrived((key, "x-", 2), into.at[:, high, xx(2)])

    def x_first(key, own, into, step):
        if step == 0:
            for dx in range(1, NX):
                send((key, "x", dx), own, into.at[:, y, x], at_x(dx))
            place_own(own, into)
        if step == 1:
            for dx in range(1, NX):
                arrived((key, "x", dx), into.at[:, y, xx(dx)])
        h = step - 1
        if 1 <= h <= 4:
            arrive = [into.at[:, yy(-h)], into.at[:, yy(h)]]
            if h == 4:
                arrive = [arrive[0].at[:, pl.ds(0, 2)], arrive[1].at[:, pl.ds(2, 2)]]
            arrived((key, "y+", h), arrive[0])
            arrived((key, "y-", h), arrive[1])
        if 0 <= h <= 3:
            up, down = (into.at[:, yy(-h)], into.at[:, yy(h)])
            if h == 3:
                up, down = (up.at[:, pl.ds(0, 2)], down.at[:, pl.ds(2, 2)])
            send((key, "y+", h + 1), up, up, at_y(1))
            send((key, "y-", h + 1), down, down, at_y(NY - 1))

    def pair_step(t, step):
        into, low, high = cuv.at[:, t], pl.ds(0, 4), pl.ds(4, 4)
        if step == 0:
            for dy in FAR_FIRST:
                send(("py", t, dy), cown.at[:, t], into.at[:, y, x], at_y(dy))
            for i in range(2):
                cuv[i, t, y, x] = cown[i, t]
        if step == 1:
            for dy in NEAR_FIRST:
                arrived(("py", t, dy), into.at[:, yy(-dy), x])
            send(("px+", t, 1), into.at[:, :, x], into.at[:, :, x], at_x(1))
            send(("px-", t, 1), into.at[:, :, x], into.at[:, :, x], at_x(NX - 1))
        if step == 2:
            arrived(("px+", t, 1), into.at[:, :, xx(1)])
            arrived(("px-", t, 1), into.at[:, :, xx(-1)])
            send(("px+", t, 2), into.at[:, low, xx(1)], into.at[:, low, xx(1)], at_x(1))
            send(("px-", t, 2), into.at[:, high, xx(-1)], into.at[:, high, xx(-1)], at_x(NX - 1))
        if step == 3:
            arrived(("px+", t, 2), into.at[:, low, xx(2)])
            arrived(("px-", t, 2), into.at[:, high, xx(2)])

    def take(name, part, step):
        if name == "p1" or name == "p3":
            pair_step(int(name[1]) // 2, step)
        else:
            i, first = (0, x_first) if part == "u" else (1, y_first)
            group = pl.ds(*OWN[name])
            first((name, part), (uown, vown)[i].at[group], (uall, vall)[i].at[group], step)

    todo = list(ORDER)
    done = set()

    def pump(count):
        for _ in range(min(count, len(todo))):
            item = todo.pop(0)
            take(item[:2], item[2], int(item[3]))
            done.add(item)

    def pump_through(name):
        last = {name + "_3"} if name[0] == "p" else {name + "u6", name + "v6"}
        while not last <= done:
            pump(1)

    def ag_send(pieces, a):
        for dz in FAR_FIRST:
            send((a, dz), pieces.at[p], pieces.at[p], at_z(dz, c))
        send((a, "f", 0), pieces.at[p], pieces.at[p], sib)

    def ag_forward(pieces, a):
        for dz in NEAR_FIRST:
            piece = pieces.at[zz(dz) * 2 + c]
            arrived((a, dz), piece)
            send((a, "f", dz), piece, piece, sib)

    def ag_finish(pieces, a):
        for dz in range(NZ):
            arrived((a, "f", dz), pieces.at[zz(dz) * 2 + 1 - c])

    stored = [owners[i] for i in range(16)]
    my_row, sib_row = stored[0], stored[0]
    holder = [jnp.int32(0) for _ in range(WIN)]
    for i in range(16):
        my_row = jnp.where(p == i, stored[i], my_row)
        sib_row = jnp.where(p + 1 - 2 * c == i, stored[i], sib_row)
        holder = [jnp.where(stored[i] == j, i, h) for j, h in enumerate(holder)]

    def scatter(j, own, other):
        square = (128, 128)
        mine = jnp.full(square, my_row, jnp.int32) == j
        sibs = jnp.full(square, sib_row, jnp.int32) == j
        for g in range(NZ):
            far = jnp.where(sibs, other[g].astype(F32), 0.0)
            comb[j, g] = jnp.where(mine, own[g, c].astype(F32), far).astype(BF16)
        for dz in FAR_FIRST:
            send(("rs", j, dz), comb.at[j, lax.rem(z + dz, NZ)], rsb.at[j, dz], at_z(dz, c))

    def scattered(j):
        total = comb[j, z].astype(F32)
        for dz in NEAR_FIRST:
            arrived(("rs", j, dz), rsb.at[j, dz])
            total = total + rsb[j, dz].astype(F32)
        nag[j, p] = total.astype(BF16)

    def solve_far(j):
        acc = jnp.zeros((128, 128), F32)
        for g in range(NZ):
            acc += dot(dchip[j, pl.ds(0, 128), pl.ds(256 * g, 256)], nag[j, pl.ds(2 * g, 2)].reshape(256, 128))
        return acc

    def store_solved(j, value):
        solved[j] = value.astype(BF16)
        xag[j, p] = value.T.astype(BF16)
        ag_send(xag.at[j], ("x", j))

    def times_solved(j, factor):
        total = None
        for g in range(NY):
            both = jnp.concatenate([xag[j, 2 * g], xag[j, 2 * g + 1]], axis=1)
            term = dot(both, factor(g))
            total = term if total is None else total + term
        return total

    def pair_term(j, k):
        t = PAIRS.index((j, k))
        coeffs = times_solved(k, lambda g: cuv[1, t, g].reshape(256, 128)).T.astype(BF16)
        total = jnp.zeros((256, 128), F32)
        for g in range(NY):
            part = dot(cuv[0, t, g].reshape(256, 128), coeffs).astype(BF16)
            total += dot(dchip[j, :, pl.ds(256 * g, 256)], part)
        return total

    def update(k):
        ct = times_solved(k, lambda g: vall[k, g].reshape(256, 256))
        keep = lax.broadcasted_iota(jnp.int32, (128, 256), 1) < jnp.where(k < my_row, ranks[0, k], 0)
        coeffs = jnp.where(keep, ct, 0.0).T.astype(BF16)
        for g in range(NY):
            old = rin[g].reshape(256, 128).astype(F32) if k == 0 else res[g]
            new = old - dot(uall[k, g].reshape(256, 256), coeffs)
            if k < WIN - 1:
                res[g] = new
            if k == 1:
                stage[g] = new.astype(BF16).reshape(2, 128, 128)
            if k == WIN - 1:
                updated[g] = new.astype(BF16).reshape(2, 128, 128)

    for load in loads[:3]:
        load.wait()
    lane = lax.broadcasted_iota(jnp.int32, (64, 128), 1)
    for t, (_, k) in enumerate(PAIRS):
        for core in range(2):
            lanes = pl.ds(128 * core, 128)
            us = uown[k, :, lanes].reshape(4, 16, 128)
            vs = vown[k, :, lanes].astype(F32)
            vs = jnp.where(lane + 128 * core < ranks[0, k], vs, 0.0).astype(BF16).reshape(4, 16, 128)
            for i in range(4):
                cout[2 * i + core, t] = us[i]
                cout[8 + 2 * i + core, t] = vs[i]

    pl.semaphore_wait(barrier, len(peers))
    send(("r", 0), rin.at[:, 1 - c], sibb.at[0], sib)
    for i, (dz, core) in enumerate(ring):
        to = lax.rem(z + dz, NZ) * 2 + core
        send(("c", i), cout.at[to], crs.at[p], at_z(dz, core))
    pump(2)
    crs[p] = cout[p]
    arrived(("r", 0), sibb.at[0])
    scatter(0, rin, sibb.at[0])
    loads[3].wait()
    near_d = [dchip.at[j, pl.ds(0, 128)] for j, _ in PAIRS]
    far_d = [dchip.at[j, pl.ds(128, 128)] for j, _ in PAIRS]
    for t in range(len(PAIRS)):
        send(("d", t), near_d[t], far_d[t], sib)
    pump(2)
    for i, (dz, core) in enumerate(ring):
        arrived(("c", i), crs.at[zz(dz) * 2 + core])
    part = pl.ds(pl.multiple_of(16 * (z % 4), 16), 16)
    for t, (j, _) in enumerate(PAIRS):
        cown[z // 4, t, part] = crs[holder[j], t]
    for dz in FAR_FIRST:
        place = cown.at[z // 4, :, part]
        send(("cag", dz), place, place, at_z(dz, c))
    pump(1)
    scattered(0)
    ag_send(nag.at[0], "n0")
    scatter(1, rin, sibb.at[0])
    pump(2)
    for dz in NEAR_FIRST:
        arrived(("cag", dz), cown.at[zz(dz) // 4, :, pl.ds(pl.multiple_of(16 * (zz(dz) % 4), 16), 16)])
    pump(2)
    ag_forward(nag.at[0], "n0")
    ag_finish(nag.at[0], "n0")
    for j in range(WIN):
        even = j % 2 == 0
        if even:
            store_solved(j, solve_far(j))
            pump(1)
            scattered(j + 1)
            ag_send(nag.at[j + 1], "n" + str(j + 1))
        pump((2, 4, 4, 0)[j])
        ag_forward(xag.at[j], ("x", j))
        pump((1, 0, 0, 0)[j])
        ag_finish(xag.at[j], ("x", j))
        if even:
            t = j // 2
            pump_through("p" + str(j + 1))
            arrived(("d", t), far_d[t])
            term = pair_term(j + 1, j)
            ysend[t] = term[128:]
            send(("y", t), ysend.at[t], yrecv.at[t], sib)
            ag_forward(nag.at[j + 1], "n" + str(j + 1))
            ag_finish(nag.at[j + 1], "n" + str(j + 1))
            known = solve_far(j + 1) - term[:128]
            arrived(("y", t), yrecv.at[t])
            store_solved(j + 1, known - yrecv[t])
            pump_through("m" + str(j))
        update(j)
        if j == 1:
            send(("r", 1), stage.at[:, 1 - c], sibb.at[1], sib)
            arrived(("r", 1), sibb.at[1])
            scatter(2, stage, sibb.at[1])
            pump(3)
            scattered(2)
            ag_send(nag.at[2], "n2")
            scatter(3, stage, sibb.at[1])
            pump(3)
            ag_forward(nag.at[2], "n2")
            ag_finish(nag.at[2], "n2")
    for copy in sent:
        copy.wait_send()


def body(rhs_blocks, left_u, left_v, tile_ranks, diag_inverse, row_owner):
    vmem, smem, hbm = (pl.BlockSpec(memory_space=s) for s in (pltpu.VMEM, pltpu.SMEM, pl.ANY))
    blocks = (NZ, 2, 128, 128)
    pairs = len(PAIRS)
    solved, updated = pl.pallas_call(
        kernel,
        out_shape=(jax.ShapeDtypeStruct((WIN, 128, 128), BF16), jax.ShapeDtypeStruct(blocks, BF16)),
        in_specs=[smem, smem, hbm, hbm, hbm, hbm],
        out_specs=(vmem, vmem),
        scratch_shapes=[
            pltpu.VMEM((WIN, NY, NX, 64, 256), BF16),
            pltpu.VMEM((WIN, NY, NX, 64, 256), BF16),
            pltpu.VMEM((2, pairs, NY, NX, 64, 128), BF16),
            pltpu.VMEM((WIN, 64, 256), BF16),
            pltpu.VMEM((WIN, 64, 256), BF16),
            pltpu.VMEM(blocks, BF16),
            pltpu.VMEM((WIN, 256, 2048), BF16),
            pltpu.VMEM((NZ, 256, 128), F32),
            pltpu.VMEM(blocks, BF16),
            pltpu.VMEM((2, NZ, 128, 128), BF16),
            pltpu.VMEM((WIN, NZ, 128, 128), BF16),
            pltpu.VMEM((WIN, NZ, 128, 128), BF16),
            pltpu.VMEM((WIN, 16, 128, 128), BF16),
            pltpu.VMEM((WIN, 16, 128, 128), BF16),
            pltpu.VMEM((16, pairs, 16, 128), BF16),
            pltpu.VMEM((16, pairs, 16, 128), BF16),
            pltpu.VMEM((2, pairs, 64, 128), BF16),
            pltpu.VMEM((pairs, 128, 128), F32),
            pltpu.VMEM((pairs, 128, 128), F32),
            pltpu.SemaphoreType.DMA((4,)),
            pltpu.SemaphoreType.DMA((400,)),
            pltpu.SemaphoreType.DMA((400,)),
        ],
        compiler_params=pltpu.CompilerParams(
            collective_id=0, has_side_effects=True, vmem_limit_bytes=62 << 20
        ),
        name="substitution",
    )(tile_ranks, row_owner, rhs_blocks.reshape(blocks), left_u, left_v, diag_inverse)
    return solved, updated.reshape(1, 2048, 128)


def solution(mesh):
    return jax.shard_map(
        body,
        mesh=mesh,
        in_specs=(
            P("rows", None, "rhs"),
            P("rows", None, "rhs", None),
            P("rows", None, "rhs", None),
            P("rows", None),
            P(None, "rows", None),
            P(),
        ),
        out_specs=(P(None, "rows", "rhs"), P("rows", None, "rhs")),
        check_vma=False,
    )
```

```python
import jax
import jax.numpy as jnp
from jax import lax
from jax.experimental import pallas as pl
from jax.experimental.pallas import tpu as pltpu
from jax.sharding import PartitionSpec as P

MESH = pl.DeviceIdType.MESH
NZ, NY, NX, WIN = 8, 8, 4, 4
FAR_FIRST = (4, 3, 5, 2, 6, 1, 7)
NEAR_FIRST = (1, 7, 2, 6, 3, 5, 4)
PAIRS = ((1, 0), (3, 2))
F32, BF16 = jnp.float32, jnp.bfloat16
OWN = {"m0": (0, 2), "m2": (2, 2)}
ORDER = (
    "m0v0", "m0u0", "m0v1", "m0u1", "m0v2", "m0v3", "m0u2", "p1_0", "m0v4", "p1_1", "m0u3", "p1_2", "m0v5", "m0u4",
    "p1_3", "m0v6", "m0u5", "m0u6", "m2v0", "m2u0", "m2v1", "m2u1", "m2v2", "m2v3", "p3_0", "m2u2", "m2v4", "p3_1",
    "m2u3", "p3_2", "m2v5", "m2u4", "p3_3", "m2v6", "m2u5", "m2u6",
)


def dot(a, b):
    return jnp.dot(a, b, preferred_element_type=F32)


def kernel(ranks, owners, rhs, u, v, d, solved, updated, uall, vall, cuv, uown, vown, rin, dchip, res,
           stage, sibb, comb, rsb, nag, xag, cout, crs, cown, ysend, yrecv, lsem, ssem, rsem):
    p, q = lax.axis_index("rows"), lax.axis_index("rhs")
    z, c, y, x = p // 2, p % 2, q // 4, q % 4

    loads = []
    for i, (src, dst) in enumerate(
        ((u.at[0], uown), (v.at[0], vown), (rhs, rin), (d, dchip.at[:, pl.ds(0, 128)]))
    ):
        load = pltpu.make_async_copy(src, dst, lsem.at[i])
        load.start()
        loads.append(load)

    def at_z(dz, core):
        return {"rows": lax.rem(z + dz, NZ) * 2 + core, "rhs": q}

    def at_y(dy):
        return {"rows": p, "rhs": lax.rem(y + dy, NY) * 4 + x}

    def at_x(dx):
        return {"rows": p, "rhs": y * 4 + lax.rem(x + dx, NX)}

    sib = at_z(0, 1 - c)
    ring = [(dz, core) for dz in FAR_FIRST for core in (c, 1 - c)] + [(0, 1 - c)]
    barrier = pltpu.get_barrier_semaphore()
    peers = [at_z(dz, core) for dz, core in ring]
    peers += [at_y(dy) for dy in range(1, NY)] + [at_x(dx) for dx in range(1, NX)]
    for peer in peers:
        pl.semaphore_signal(barrier, inc=1, device_id=peer, device_id_type=MESH)

    numbers, sent = {}, []

    def copy_of(key, src, dst, peer):
        n = numbers.setdefault(key, len(numbers))
        return pltpu.make_async_remote_copy(
            src_ref=src, dst_ref=dst, send_sem=ssem.at[n], recv_sem=rsem.at[n], device_id=peer, device_id_type=MESH
        )

    def send(key, src, dst, peer):
        copy = copy_of(key, src, dst, peer)
        copy.start()
        sent.append(copy)

    def arrived(key, dst):
        copy_of(key, dst, dst, sib).wait_recv()

    def zz(dz):
        return lax.rem(z + NZ - dz, NZ)

    def yy(dy):
        return lax.rem(y + dy + NY, NY)

    def xx(dx):
        return lax.rem(x + NX - dx, NX)

    def place_own(own, into):
        for i in range(own.shape[0]):
            into[i, y, x] = own[i]

    def y_first(key, own, into, step):
        if step == 0:
            place_own(own, into)
        if 1 <= step <= 4:
            arrive = [into.at[:, yy(-step), x], into.at[:, yy(step), x]]
            if step == 4:
                arrive = [arrive[0].at[:, pl.ds(0, 32)], arrive[1].at[:, pl.ds(32, 32)]]
            arrived((key, "y+", step), arrive[0])
            arrived((key, "y-", step), arrive[1])
        if step <= 3:
            up, down = (into.at[:, yy(-step), x], into.at[:, yy(step), x])
            if step == 3:
                up, down = (up.at[:, pl.ds(0, 32)], down.at[:, pl.ds(32, 32)])
            send((key, "y+", step + 1), up, up, at_y(1))
            send((key, "y-", step + 1), down, down, at_y(NY - 1))
        if step == 4:
            send((key, "x+", 1), into.at[:, :, x], into.at[:, :, x], at_x(1))
            send((key, "x-", 1), into.at[:, :, x], into.at[:, :, x], at_x(NX - 1))
        low, high = pl.ds(0, 4), pl.ds(4, 4)
        if step == 5:
            arrived((key, "x+", 1), into.at[:, :, xx(1)])
            arrived((key, "x-", 1), into.at[:, :, xx(-1)])
            send((key, "x+", 2), into.at[:, low, xx(1)], into.at[:, low, xx(1)], at_x(1))
            send((key, "x-", 2), into.at[:, high, xx(-1)], into.at[:, high, xx(-1)], at_x(NX - 1))
        if step == 6:
            arrived((key, "x+", 2), into.at[:, low, xx(2)])
            arrived((key, "x-", 2), into.at[:, high, xx(2)])

    def x_first(key, own, into, step):
        if step == 0:
            for dx in range(1, NX):
                send((key, "x", dx), own, into.at[:, y, x], at_x(dx))
            place_own(own, into)
        if step == 1:
            for dx in range(1, NX):
                arrived((key, "x", dx), into.at[:, y, xx(dx)])
        h = step - 1
        if 1 <= h <= 4:
            arrive = [into.at[:, yy(-h)], into.at[:, yy(h)]]
            if h == 4:
                arrive = [arrive[0].at[:, pl.ds(0, 2)], arrive[1].at[:, pl.ds(2, 2)]]
            arrived((key, "y+", h), arrive[0])
            arrived((key, "y-", h), arrive[1])
        if 0 <= h <= 3:
            up, down = (into.at[:, yy(-h)], into.at[:, yy(h)])
            if h == 3:
                up, down = (up.at[:, pl.ds(0, 2)], down.at[:, pl.ds(2, 2)])
            send((key, "y+", h + 1), up, up, at_y(1))
            send((key, "y-", h + 1), down, down, at_y(NY - 1))

    def pair_step(t, step):
        into, low, high = cuv.at[:, t], pl.ds(0, 4), pl.ds(4, 4)
        if step == 0:
            for dy in FAR_FIRST:
                send(("py", t, dy), cown.at[:, t], into.at[:, y, x], at_y(dy))
            for i in range(2):
                cuv[i, t, y, x] = cown[i, t]
        if step == 1:
            for dy in NEAR_FIRST:
                arrived(("py", t, dy), into.at[:, yy(-dy), x])
            send(("px+", t, 1), into.at[:, :, x], into.at[:, :, x], at_x(1))
            send(("px-", t, 1), into.at[:, :, x], into.at[:, :, x], at_x(NX - 1))
        if step == 2:
            arrived(("px+", t, 1), into.at[:, :, xx(1)])
            arrived(("px-", t, 1), into.at[:, :, xx(-1)])
            send(("px+", t, 2), into.at[:, low, xx(1)], into.at[:, low, xx(1)], at_x(1))
            send(("px-", t, 2), into.at[:, high, xx(-1)], into.at[:, high, xx(-1)], at_x(NX - 1))
        if step == 3:
            arrived(("px+", t, 2), into.at[:, low, xx(2)])
            arrived(("px-", t, 2), into.at[:, high, xx(2)])

    def take(name, part, step):
        if name == "p1" or name == "p3":
            pair_step(int(name[1]) // 2, step)
        else:
            i, first = (0, x_first) if part == "u" else (1, y_first)
            group = pl.ds(*OWN[name])
            first((name, part), (uown, vown)[i].at[group], (uall, vall)[i].at[group], step)

    todo = list(ORDER)
    done = set()

    def pump(count):
        for _ in range(min(count, len(todo))):
            item = todo.pop(0)
            take(item[:2], item[2], int(item[3]))
            done.add(item)

    def pump_through(name):
        last = {name + "_3"} if name[0] == "p" else {name + "u6", name + "v6"}
        while not last <= done:
            pump(1)

    def ag_send(pieces, a):
        for dz in FAR_FIRST:
            send((a, dz), pieces.at[p], pieces.at[p], at_z(dz, c))
        send((a, "f", 0), pieces.at[p], pieces.at[p], sib)

    def ag_forward(pieces, a):
        for dz in NEAR_FIRST:
            piece = pieces.at[zz(dz) * 2 + c]
            arrived((a, dz), piece)
            send((a, "f", dz), piece, piece, sib)

    def ag_finish(pieces, a):
        for dz in range(NZ):
            arrived((a, "f", dz), pieces.at[zz(dz) * 2 + 1 - c])

    stored = [owners[i] for i in range(16)]
    my_row, sib_row = stored[0], stored[0]
    holder = [jnp.int32(0) for _ in range(WIN)]
    for i in range(16):
        my_row = jnp.where(p == i, stored[i], my_row)
        sib_row = jnp.where(p + 1 - 2 * c == i, stored[i], sib_row)
        holder = [jnp.where(stored[i] == j, i, h) for j, h in enumerate(holder)]

    def scatter(j, own, other):
        square = (128, 128)
        mine = jnp.full(square, my_row, jnp.int32) == j
        sibs = jnp.full(square, sib_row, jnp.int32) == j
        for g in range(NZ):
            far = jnp.where(sibs, other[g].astype(F32), 0.0)
            comb[j, g] = jnp.where(mine, own[g, c].astype(F32), far).astype(BF16)
        for dz in FAR_FIRST:
            send(("rs", j, dz), comb.at[j, lax.rem(z + dz, NZ)], rsb.at[j, dz], at_z(dz, c))

    def scattered(j):
        total = comb[j, z].astype(F32)
        for dz in NEAR_FIRST:
            arrived(("rs", j, dz), rsb.at[j, dz])
            total = total + rsb[j, dz].astype(F32)
        nag[j, p] = total.astype(BF16)

    def solve_far(j):
        acc = jnp.zeros((128, 128), F32)
        for g in range(NZ):
            acc += dot(dchip[j, pl.ds(0, 128), pl.ds(256 * g, 256)], nag[j, pl.ds(2 * g, 2)].reshape(256, 128))
        return acc

    def store_solved(j, value):
        solved[j] = value.astype(BF16)
        xag[j, p] = value.T.astype(BF16)
        ag_send(xag.at[j], ("x", j))

    def times_solved(j, factor):
        total = None
        for g in range(NY):
            both = jnp.concatenate([xag[j, 2 * g], xag[j, 2 * g + 1]], axis=1)
            term = dot(both, factor(g))
            total = term if total is None else total + term
        return total

    def pair_term(j, k):
        t = PAIRS.index((j, k))
        coeffs = times_solved(k, lambda g: cuv[1, t, g].reshape(256, 128)).T.astype(BF16)
        total = jnp.zeros((256, 128), F32)
        for g in range(NY):
            part = dot(cuv[0, t, g].reshape(256, 128), coeffs).astype(BF16)
            total += dot(dchip[j, :, pl.ds(256 * g, 256)], part)
        return total

    def update(k):
        ct = times_solved(k, lambda g: vall[k, g].reshape(256, 256))
        keep = lax.broadcasted_iota(jnp.int32, (128, 256), 1) < jnp.where(k < my_row, ranks[0, k], 0)
        coeffs = jnp.where(keep, ct, 0.0).T.astype(BF16)
        for g in range(NY):
            old = rin[g].reshape(256, 128).astype(F32) if k == 0 else res[g]
            new = old - dot(uall[k, g].reshape(256, 256), coeffs)
            if k < WIN - 1:
                res[g] = new
            if k == 1:
                stage[g] = new.astype(BF16).reshape(2, 128, 128)
            if k == WIN - 1:
                updated[g] = new.astype(BF16).reshape(2, 128, 128)

    for load in loads[:3]:
        load.wait()
    lane = lax.broadcasted_iota(jnp.int32, (64, 128), 1)
    for t, (_, k) in enumerate(PAIRS):
        for core in range(2):
            lanes = pl.ds(128 * core, 128)
            us = uown[k, :, lanes].reshape(4, 16, 128)
            vs = vown[k, :, lanes].astype(F32)
            vs = jnp.where(lane + 128 * core < ranks[0, k], vs, 0.0).astype(BF16).reshape(4, 16, 128)
            for i in range(4):
                cout[2 * i + core, t] = us[i]
                cout[8 + 2 * i + core, t] = vs[i]

    pl.semaphore_wait(barrier, len(peers))
    send(("r", 0), rin.at[:, 1 - c], sibb.at[0], sib)
    for i, (dz, core) in enumerate(ring):
        to = lax.rem(z + dz, NZ) * 2 + core
        send(("c", i), cout.at[to], crs.at[p], at_z(dz, core))
    pump(2)
    crs[p] = cout[p]
    arrived(("r", 0), sibb.at[0])
    scatter(0, rin, sibb.at[0])
    loads[3].wait()
    near_d = [dchip.at[j, pl.ds(0, 128)] for j, _ in PAIRS]
    far_d = [dchip.at[j, pl.ds(128, 128)] for j, _ in PAIRS]
    for t in range(len(PAIRS)):
        send(("d", t), near_d[t], far_d[t], sib)
    pump(2)
    for i, (dz, core) in enumerate(ring):
        arrived(("c", i), crs.at[zz(dz) * 2 + core])
    part = pl.ds(pl.multiple_of(16 * (z % 4), 16), 16)
    for t, (j, _) in enumerate(PAIRS):
        cown[z // 4, t, part] = crs[holder[j], t]
    for dz in FAR_FIRST:
        place = cown.at[z // 4, :, part]
        send(("cag", dz), place, place, at_z(dz, c))
    pump(1)
    scattered(0)
    ag_send(nag.at[0], "n0")
    scatter(1, rin, sibb.at[0])
    pump(2)
    for dz in NEAR_FIRST:
        arrived(("cag", dz), cown.at[zz(dz) // 4, :, pl.ds(pl.multiple_of(16 * (zz(dz) % 4), 16), 16)])
    pump(2)
    ag_forward(nag.at[0], "n0")
    ag_finish(nag.at[0], "n0")
    for j in range(WIN):
        even = j % 2 == 0
        if even:
            store_solved(j, solve_far(j))
            pump(1)
            scattered(j + 1)
            ag_send(nag.at[j + 1], "n" + str(j + 1))
        pump((2, 4, 4, 0)[j])
        ag_forward(xag.at[j], ("x", j))
        pump((1, 0, 0, 0)[j])
        ag_finish(xag.at[j], ("x", j))
        if even:
            t = j // 2
            pump_through("p" + str(j + 1))
            arrived(("d", t), far_d[t])
            term = pair_term(j + 1, j)
            ysend[t] = term[128:]
            send(("y", t), ysend.at[t], yrecv.at[t], sib)
            ag_forward(nag.at[j + 1], "n" + str(j + 1))
            ag_finish(nag.at[j + 1], "n" + str(j + 1))
            known = solve_far(j + 1) - term[:128]
            arrived(("y", t), yrecv.at[t])
            store_solved(j + 1, known - yrecv[t])
            pump_through("m" + str(j))
        update(j)
        if j == 1:
            send(("r", 1), stage.at[:, 1 - c], sibb.at[1], sib)
            arrived(("r", 1), sibb.at[1])
            scatter(2, stage, sibb.at[1])
            pump(3)
            scattered(2)
            ag_send(nag.at[2], "n2")
            scatter(3, stage, sibb.at[1])
            pump(3)
            ag_forward(nag.at[2], "n2")
            ag_finish(nag.at[2], "n2")
    for copy in sent:
        copy.wait_send()


def body(rhs_blocks, left_u, left_v, tile_ranks, diag_inverse, row_owner):
    vmem, smem, hbm = (pl.BlockSpec(memory_space=s) for s in (pltpu.VMEM, pltpu.SMEM, pl.ANY))
    blocks = (NZ, 2, 128, 128)
    pairs = len(PAIRS)
    solved, updated = pl.pallas_call(
        kernel,
        out_shape=(jax.ShapeDtypeStruct((WIN, 128, 128), BF16), jax.ShapeDtypeStruct(blocks, BF16)),
        in_specs=[smem, smem, hbm, hbm, hbm, hbm],
        out_specs=(vmem, vmem),
        scratch_shapes=[
            pltpu.VMEM((WIN, NY, NX, 64, 256), BF16),
            pltpu.VMEM((WIN, NY, NX, 64, 256), BF16),
            pltpu.VMEM((2, pairs, NY, NX, 64, 128), BF16),
            pltpu.VMEM((WIN, 64, 256), BF16),
            pltpu.VMEM((WIN, 64, 256), BF16),
            pltpu.VMEM(blocks, BF16),
            pltpu.VMEM((WIN, 256, 2048), BF16),
            pltpu.VMEM((NZ, 256, 128), F32),
            pltpu.VMEM(blocks, BF16),
            pltpu.VMEM((2, NZ, 128, 128), BF16),
            pltpu.VMEM((WIN, NZ, 128, 128), BF16),
            pltpu.VMEM((WIN, NZ, 128, 128), BF16),
            pltpu.VMEM((WIN, 16, 128, 128), BF16),
            pltpu.VMEM((WIN, 16, 128, 128), BF16),
            pltpu.VMEM((16, pairs, 16, 128), BF16),
            pltpu.VMEM((16, pairs, 16, 128), BF16),
            pltpu.VMEM((2, pairs, 64, 128), BF16),
            pltpu.VMEM((pairs, 128, 128), F32),
            pltpu.VMEM((pairs, 128, 128), F32),
            pltpu.SemaphoreType.DMA((4,)),
            pltpu.SemaphoreType.DMA((400,)),
            pltpu.SemaphoreType.DMA((400,)),
        ],
        compiler_params=pltpu.CompilerParams(
            collective_id=0, has_side_effects=True, vmem_limit_bytes=62 << 20
        ),
        name="substitution",
    )(tile_ranks, row_owner, rhs_blocks.reshape(blocks), left_u, left_v, diag_inverse)
    return solved, updated.reshape(1, 2048, 128)


def solution(mesh):
    return jax.shard_map(
        body,
        mesh=mesh,
        in_specs=(
            P("rows", None, "rhs"),
            P("rows", None, "rhs", None),
            P("rows", None, "rhs", None),
            P("rows", None),
            P(None, "rows", None),
            P(),
        ),
        out_specs=(P(None, "rows", "rhs"), P("rows", None, "rhs")),
        check_vma=False,
    )
```
